32 devices in a mesh: dp: 2 (over x), ctx: 4 (over y, core), tp: 4 (over z).
Axes of the slice: x: 2, y: 2, z: 4, core: 2. Of those that a mesh axis runs over, the one named last changes fastest.
Arguments:
- tokens: bfloat16 [8192, 768], P(('dp', 'ctx')), may hold values from -6 to 6
- w_query: bfloat16 [768, 768], P('dp', 'tp'), may hold values from -0.3125 to 0.3125
- w_key: bfloat16 [768, 768], P('dp', 'tp'), may hold values from -0.3125 to 0.3125
- w_value: bfloat16 [768, 768], P('dp', 'tp'), may hold values from -0.21875 to 0.21875
- w_out: bfloat16 [768, 768], P('tp', 'dp'), may hold values from -1.75 to 1.75
- w_act: bfloat16 [768, 1152], P('dp', 'tp'), may hold values from -0.21875 to 0.21875
- w_up: bfloat16 [768, 1152], P('dp', 'tp'), may hold values from -0.21875 to 0.21875
- w_down: bfloat16 [1152, 768], P('tp', 'dp'), may hold values from -0.1875 to 0.1875
- gain_one: bfloat16 [768], P('dp'), may hold values from 0.5 to 1.5
- gain_two: bfloat16 [768], P('dp'), may hold values from 0.5 to 1.5
- cotangent: bfloat16 [8192, 768], P(('dp', 'ctx')), may hold values from -6 to 6
Outputs:
- outputs: bfloat16 [8192, 768], P(('dp', 'ctx', 'tp'))
- input_grad: bfloat16 [8192, 768], P(('dp', 'ctx', 'tp'))
- grad_query: float32 [768, 768], P('dp', 'tp')
- grad_key: float32 [768, 768], P('dp', 'tp')
- grad_value: float32 [768, 768], P('dp', 'tp')
- grad_out: float32 [768, 768], P('tp', 'dp')
- grad_act: float32 [768, 1152], P('dp', 'tp')
- grad_up: float32 [768, 1152], P('dp', 'tp')
- grad_down: float32 [1152, 768], P('tp', 'dp')
- grad_gain_one: float32 [768], P('dp')
- grad_gain_two: float32 [768], P('dp')
The draws below stay inside these ranges and needn't reach their ends.
All inputs are finite; a program needn't handle non-finite values.
Results may differ from the reference program's by a relative error of at most 0.024.
Values may be sent and summed in bfloat16 or wider, within the bound.
A program may use at most 128 MiB of HBM per device.

```python
import math
import jax
import jax.numpy as jnp
from jax import lax

D = 768
HEADS = 12
HEAD = 64
FF = 1152
LEN = 4096
SEQS = 2
TOKENS = 8192


def spiked(drawn, own_key, source, target, blocks, factor):
    def block_of(dim):
        return (jnp.arange(drawn.shape[dim]) // (drawn.shape[dim] // blocks)).reshape((-1,) + (1,) * (drawn.ndim - 1 - dim))

    first = jax.random.permutation(own_key, blocks)[block_of(target)]
    far = (block_of(target) + blocks // 2) % blocks
    return jnp.where((block_of(source) == first) | (block_of(source) == far), factor * drawn, drawn)


def block_levels(key, extent, split, smallest, largest):
    def one(axis_at, parts):
        heights = jax.random.uniform(jax.random.fold_in(jax.random.fold_in(key, 6), axis_at), (parts,), jnp.float32, smallest / len(split), largest / len(split))
        return jnp.repeat(jnp.exp(heights), extent[axis_at] // parts).reshape((-1,) + (1,) * (len(extent) - axis_at - 1))

    loudness = one(*split[0])
    for cut in split[1:]:
        loudness = loudness * one(*cut)
    return loudness


def gaussian(own_key, shape, width, reach, pieces=(), held_as=jnp.bfloat16):
    loudness = block_levels(own_key, shape, pieces, -0.22, 0.18) if pieces else 1.0
    array = jax.random.normal(own_key, shape, jnp.float32) * width * loudness
    return jnp.minimum(jnp.maximum(array, -reach), reach).astype(held_as)


def noise_with(key, dims, scale, most, shards, heavy, dtype=jnp.bfloat16):
    values = scale * jax.random.normal(key, dims, jnp.float32)
    if shards:
        values = values * block_levels(key, dims, shards, -0.22, 0.18)
    return jnp.clip(spiked(values, jax.random.fold_in(key, 3), *heavy), -most, most).astype(dtype)


def setup_inputs(seed: int = 0) -> dict:
    arg_keys = jax.random.split(jax.random.key(seed), 12)
    return {
        "tokens": noise_with(arg_keys[0], (TOKENS, D), 1.0, 6.0, ((0, 8),), (0, 1, 8, 2.0)),
        "w_query": gaussian(arg_keys[1], (D, D), (D // 2) ** -0.5, 0.3125, ((0, 2), (1, 4))),
        "w_key": gaussian(arg_keys[2], (D, D), (D // 2) ** -0.5, 0.3125, ((0, 2), (1, 4))),
        "w_value": gaussian(arg_keys[3], (D, D), D ** -0.5, 0.21875, ((0, 2), (1, 4))),
        "w_out": gaussian(arg_keys[4], (D, D), (D // 64) ** -0.5, 1.75, ((0, 4), (1, 2))),
        "w_act": gaussian(arg_keys[5], (D, FF), D ** -0.5, 0.21875, ((0, 2), (1, 4))),
        "w_up": gaussian(arg_keys[6], (D, FF), D ** -0.5, 0.21875, ((0, 2), (1, 4))),
        "w_down": gaussian(arg_keys[7], (FF, D), FF ** -0.5, 0.1875, ((0, 4), (1, 2))),
        "gain_one": jnp.clip(1.0 + 0.1 * jax.random.normal(arg_keys[8], (D,), jnp.float32), 0.5, 1.5).astype(jnp.bfloat16),
        "gain_two": jnp.clip(1.0 + 0.1 * jax.random.normal(arg_keys[9], (D,), jnp.float32), 0.5, 1.5).astype(jnp.bfloat16),
        "cotangent": noise_with(arg_keys[10], (TOKENS, D), 1.0, 6.0, ((0, 8),), (0, 1, 8, 2.0)),
    }


EPSILON = 1e-05
ROPE_BASE = 160000.0
HIGHEST = lax.Precision.HIGHEST

@jax.custom_vjp
def low(v):
    return lax.optimization_barrier(v.astype(jnp.bfloat16)).astype(jnp.float32)

@jax.custom_vjp
def low_back(v):
    return v

def low_keep(v):
    return (low(v), None)

def low_pass(kept, grad):
    return (grad,)

def back_keep(v):
    return (v, None)

def back_low(kept, grad):
    return (low(grad),)
low.defvjp(low_keep, low_pass)
low_back.defvjp(back_keep, back_low)

def layer_norm(values_in, gain_vec):
    mean_value = lax.optimization_barrier(jnp.mean(values_in, axis=-1, keepdims=True))
    centred = values_in - mean_value
    spread = lax.optimization_barrier(jnp.mean(centred * centred, axis=-1, keepdims=True))
    return centred * lax.rsqrt(spread + EPSILON) * gain_vec

def rotate(tensor):
    half_size = tensor.shape[-1] // 2
    return jnp.concatenate([-tensor[..., half_size:], tensor[..., :half_size]], axis=-1)

def rotary(tensor, cosine_table, sine_table):
    return tensor * cosine_table + rotate(tensor) * sine_table

def tables(length, head_size):
    position = jnp.arange(length).astype(jnp.float32)
    frequency = ROPE_BASE ** (-jnp.arange(0, head_size, 2).astype(jnp.float32) / head_size)
    angles = position[:, None] * frequency[None, :]
    angles = jnp.concatenate([angles, angles], axis=1)
    return (jnp.cos(angles)[:, None, :], jnp.sin(angles)[:, None, :])

def project(operand, weights):
    return jnp.dot(operand, weights, precision=HIGHEST, preferred_element_type=jnp.float32)

def attention(queries, key_data, value_data):
    length = queries.shape[0]
    block_rows = math.gcd(length, 512)
    blocks = queries.reshape(length // block_rows, block_rows, HEADS, HEAD)

    @jax.checkpoint
    def query_block(block_queries):
        raw_scores = jnp.einsum('qhd,khd->hqk', block_queries, key_data, precision=HIGHEST)
        scores = low_back(raw_scores) * HEAD ** (-0.5)
        weights = low(jnp.exp(scores - jax.nn.logsumexp(scores, axis=-1, keepdims=True)))
        return jnp.einsum('hqk,khd->qhd', weights, value_data, precision=HIGHEST)
    return lax.map(query_block, blocks).reshape(length, HEADS * HEAD)

def encoder_layer(inputs, w_query, w_key, w_value, w_out, w_act, w_up, w_down, gain_one, gain_two):
    length = inputs.shape[0]
    cosine_table, sine_table = tables(length, HEAD)
    normed = low(layer_norm(inputs, gain_one))
    queries = low(rotary(low_back(project(normed, w_query)).reshape(length, HEADS, HEAD), cosine_table, sine_table))
    key_data = low(rotary(low_back(project(normed, w_key)).reshape(length, HEADS, HEAD), cosine_table, sine_table))
    value_data = low(low_back(project(normed, w_value))).reshape(length, HEADS, HEAD)
    mixed = low(low_back(attention(queries, key_data, value_data)))
    middle = inputs + low_back(project(mixed, w_out))
    normed_two = low(layer_norm(middle, gain_two))
    gate_pre = low_back(project(normed_two, w_act))
    up_pre = low_back(project(normed_two, w_up))
    hidden = low(jax.nn.gelu(gate_pre, approximate=False) * up_pre)
    return middle + low_back(project(hidden, w_down))

def reference(tokens, w_query, w_key, w_value, w_out, w_act, w_up, w_down, gain_one, gain_two, cotangent):
    weight_list = tuple((item.astype(jnp.float32) for item in (w_query, w_key, w_value, w_out, w_act, w_up, w_down, gain_one, gain_two)))
    inputs = tokens.astype(jnp.float32).reshape(SEQS, LEN, D)
    cot_rows = cotangent.astype(jnp.float32).reshape(SEQS, LEN, D)

    def one_sequence(running, sequence_pair):
        seq_inputs, seq_cot = sequence_pair
        result, pullback = jax.vjp(encoder_layer, seq_inputs, *weight_list)
        gradients = pullback(seq_cot)
        return (tuple((left_sum + right_sum for left_sum, right_sum in zip(running, gradients[1:]))), (result, gradients[0]))
    initial = tuple((jnp.zeros_like(item) for item in weight_list))
    sums, (results, input_grads) = lax.scan(one_sequence, initial, (inputs, cot_rows))
    return (results.reshape(TOKENS, D).astype(jnp.bfloat16), input_grads.reshape(TOKENS, D).astype(jnp.bfloat16), sums[0], sums[1], sums[2], sums[3], sums[4], sums[5], sums[6], sums[7], sums[8])
```

```python
import functools
import math

import jax
import jax.numpy as jnp
import numpy as np
from jax import lax
from jax.experimental import pallas as pl
from jax.experimental.pallas import tpu as pltpu
from jax.sharding import PartitionSpec as P

HEAD = 64
EPSILON = 1e-05
ROPE_BASE = 160000.0
MESH = pl.DeviceIdType.MESH
BF = jnp.bfloat16
F32 = jnp.float32
VM = pl.BlockSpec(memory_space=pltpu.VMEM)


def nn(a, b):
    return lax.dot_general(a, b, (((1,), (0,)), ((), ())), preferred_element_type=F32)


def nt(a, b):
    return lax.dot_general(a, b, (((1,), (1,)), ((), ())), preferred_element_type=F32)


def tn(a, b):
    return lax.dot_general(a, b, (((0,), (0,)), ((), ())), preferred_element_type=F32)


def iotas(rows, cols):
    return (
        lax.broadcasted_iota(jnp.int32, (rows, cols), 0),
        lax.broadcasted_iota(jnp.int32, (rows, cols), 1),
    )


def spread(rows, cols, shift):
    i, j = iotas(rows, cols)
    return (j == (i // HEAD) * 128 + i % HEAD + shift).astype(BF)


def gather_cols(rows, cols, shift):
    i, j = iotas(rows, cols)
    return (i == (j // HEAD) * 128 + j % HEAD + shift).astype(BF)


def turn(back):
    i, j = iotas(128, 128)
    if back:
        i, j = j, i
    half = HEAD // 2
    plus = (i == j - half) & (j < HEAD)
    minus = (i == j + half) & (i < HEAD)
    return jnp.where(plus, 1.0, jnp.where(minus, -1.0, 0.0)).astype(BF)


def turned(z, r):
    high = z.astype(BF)
    rest = (z - high.astype(F32)).astype(BF)
    return nn(high, r) + nn(rest, r)


def standardize(x):
    mean_value = jnp.mean(x, axis=-1, keepdims=True)
    centred = x - mean_value
    inverse = lax.rsqrt(jnp.mean(centred * centred, axis=-1, keepdims=True) + EPSILON)
    return centred * inverse, inverse


def norm_back(grad_hat, hat, inverse):
    mean_grad = jnp.mean(grad_hat, axis=-1, keepdims=True)
    mean_cross = jnp.mean(grad_hat * hat, axis=-1, keepdims=True)
    return inverse * (grad_hat - mean_grad - hat * mean_cross)


def greet(peers):
    barrier = pltpu.get_barrier_semaphore()
    for peer in peers:
        pl.semaphore_signal(barrier, inc=1, device_id=peer, device_id_type=MESH)
    pl.semaphore_wait(barrier, len(peers))


def send(src, dst, s_sem, r_sem, peer):
    copy = pltpu.make_async_remote_copy(
        src_ref=src, dst_ref=dst, send_sem=s_sem, recv_sem=r_sem, device_id=peer, device_id_type=MESH
    )
    copy.start()
    return copy


def ring(axis, count):
    me = lax.axis_index(axis)
    return [lax.rem(me + o, count) for o in range(1, count)]


def pairs(dp, ctx):
    d, c = lax.axis_index("dp"), lax.axis_index("ctx")
    return [
        (lax.rem(d + od, dp), lax.rem(c + oc, ctx))
        for od in range(dp)
        for oc in range(ctx)
        if od or oc
    ]


def project_kernel(
    dp, tok, pa, gn, tab, q_out, kv_out, wa, gf, n1, gslot, wq2, gs, gr, ws, wr
):
    rows = tok.shape[0]
    width = tok.shape[1]
    part = pa.shape[0]
    me = lax.axis_index("dp")
    peers = ring("dp", dp)
    greet([{"dp": p} for p in peers])
    copies = []
    for o, p in enumerate(peers):
        copies.append(send(gn, gslot.at[me], gs.at[o], gr.at[o], {"dp": p}))
    weights = []
    for o, p in enumerate(peers):
        weights.append(send(pa, wa.at[me], ws.at[o], wr.at[o], {"dp": p}))
    wa[me] = pa[...]
    gslot[me] = gn[...]
    for c in copies:
        c.wait()
    gains = jnp.zeros((16, width), F32)
    for d in range(dp):
        i, j = iotas(part, width)
        gains = gains + nn(gslot[d], (j == i + d * part).astype(BF))
    gf[...] = gains

    def norm_rows(i, carry):
        at = pl.ds(pl.multiple_of(i * 128, 128), 128)
        hat, _ = standardize(tok[at, :].astype(F32))
        n1[at, :] = (hat * gf[0:1, :]).astype(BF)
        return carry

    lax.fori_loop(0, rows // 128, norm_rows, 0)
    for c in weights:
        c.wait()
    whole = wa[...].reshape(width, wa.shape[2])
    wq2[...] = nn(whole[:, :256], spread(256, 384, 0)).astype(BF)
    r = turn(False)

    def chunk(i, carry):
        at = pl.ds(pl.multiple_of(i * 256, 256), 256)
        x = n1[at, :]
        zq = nn(x, wq2[...])
        zk = nn(x, wa[...].reshape(width, wa.shape[2])[:, 256:])
        cosine, sine = tab[at, 0:128], tab[at, 128:256]
        for h in range(3):
            a = zq[:, h * 128 : (h + 1) * 128]
            q_out[h, at, :] = (0.125 * (a * cosine + turned(a, r) * sine)).astype(BF)
            b = zk[:, h * 128 : (h + 1) * 128]
            kv_out[h, at, :] = (b * cosine + turned(b, r) * sine).astype(BF)
        return carry

    lax.fori_loop(0, rows // 256, chunk, 0)


def attend_kernel(
    dp, tp, q, kv, pb, pc, kvall, mixall, mixf, lse, wb, wo,
    m_s, l_s, acc, vt, ks, kr, bs, br, cs, cr, ts, tr,
):
    rows = q.shape[1]
    d, c, t = lax.axis_index("dp"), lax.axis_index("ctx"), lax.axis_index("tp")
    sib = c + 1 - 2 * lax.rem(c, 2)
    far = lax.rem(c + 2, 4)
    diag = lax.rem(sib + 2, 4)
    dps = ring("dp", dp)
    both = [
        (lax.rem(d + od, dp), lax.rem(t + ot, tp))
        for od in range(dp)
        for ot in range(tp)
        if od or ot
    ]
    greet(
        [{"ctx": sib}, {"ctx": far}] + [{"dp": a, "tp": b} for a, b in both]
    )
    to_far = send(kv, kvall.at[c], ks.at[1], kr.at[1], {"ctx": far})
    to_sib = send(kv, kvall.at[c], ks.at[0], kr.at[0], {"ctx": sib})
    copies = []
    for o, (a, b) in enumerate(both):
        copies.append(send(pc, wo.at[t, d], cs.at[o], cr.at[o], {"dp": a, "tp": b}))
    for o, a in enumerate(dps):
        copies.append(send(pb, wb.at[d], bs.at[o], br.at[o], {"dp": a}))
    wo[t, d] = pc[...]
    wb[d] = pb[...]
    kvall[c] = kv[...]
    m_s[...] = jnp.full(m_s.shape, -1e30, F32)
    l_s[...] = jnp.zeros(l_s.shape, F32)
    acc[...] = jnp.zeros(acc.shape, F32)
    tps = ring("tp", tp)

    def block(step, b):
        def per_head(h, carry):
            vt[...] = kvall[b, h][:, HEAD:].T

            def per_tile(i, inner):
                at = pl.ds(pl.multiple_of(i * 256, 256), 256)
                s = nt(kvall[b, h], q[h, at, :])
                old = m_s[h, 0:1, at]
                new = jnp.maximum(old, jnp.max(s, axis=0, keepdims=True))
                p = jnp.exp(s - new)
                shrink = jnp.exp(old - new)
                m_s[h, 0:1, at] = new
                total = l_s[h, 0:1, at] * shrink + jnp.sum(p, axis=0, keepdims=True)
                l_s[h, 0:1, at] = total
                fresh = acc[h, :, at] * shrink + nn(vt[...], p.astype(BF))
                if step < 3:
                    acc[h, :, at] = fresh
                else:
                    mix = fresh / total
                    mixf[h, :, at] = mix
                    mixall[t, h, :, at] = mix.astype(BF)
                    lse[h, :, at] = jnp.broadcast_to(new + jnp.log(total), (8, 256))
                return inner

            lax.fori_loop(0, rows // 256, per_tile, 0)
            if step == 3:
                for o, p in enumerate(tps):
                    send(
                        mixall.at[t, h], mixall.at[t, h], ts.at[o, h], tr.at[o, h], {"tp": p}
                    )
            return carry

        lax.fori_loop(0, 3, per_head, 0)

    block(0, c)
    to_sib.wait_recv()
    block(1, sib)
    to_far.wait_recv()
    onward = send(kvall.at[far], kvall.at[far], ks.at[2], kr.at[2], {"ctx": sib})
    block(2, far)
    onward.wait_recv()
    block(3, diag)
    to_far.wait_send()
    to_sib.wait_send()
    onward.wait_send()
    for x in copies:
        x.wait()
    for h in range(3):
        for o, p in enumerate(tps):
            pltpu.make_async_remote_copy(
                src_ref=mixall.at[t, h], dst_ref=mixall.at[t, h], send_sem=ts.at[o, h],
                recv_sem=tr.at[o, h], device_id={"tp": p}, device_id_type=MESH,
            ).wait()


def feed_kernel(
    tp, tok, mixall, wo, wb, gf, cot, outp, mid_rows, gm_rows, g128, gall, gain2,
    n2, ggu, hid, gnp, gnr, gml, ss, sr, as_, ar,
):
    rows, width = tok.shape
    unit = rows // tp
    t = lax.axis_index("tp")
    tps = ring("tp", tp)
    greet([{"tp": p} for p in tps])

    def chunk(i, carry):
        c = lax.rem(t + 1 + i, tp)
        at = pl.ds(pl.multiple_of(c * unit, unit), unit)
        middle = tok[at, :].astype(F32)
        for k in range(tp):
            m = mixall[k, :, :, at].reshape(wo.shape[2], unit).T
            middle = middle + nt(m, wo[k])
        mid_rows[...] = middle
        hat, _ = standardize(middle)
        x = (hat * gf[1:2, :]).astype(BF)
        n2[at, :] = x
        w_act, w_up, w_down = wb[0], wb[1], wb[2]
        gate = nn(x, w_act)
        up = nn(x, w_up)
        gh = nn(cot[at, :], w_down)
        cdf = 0.5 * (1.0 + lax.erf(gate * (1.0 / math.sqrt(2.0))))
        density = jnp.exp(-0.5 * gate * gate) * (1.0 / math.sqrt(2.0 * math.pi))
        active = gate * cdf
        hidden = (active * up).astype(BF)
        hid[at, :] = hidden
        gg = (gh * up * (cdf + gate * density)).astype(BF)
        gu = (gh * active).astype(BF)
        ggu[0, at, :] = gg
        ggu[1, at, :] = gu
        gnp[c] = (nt(gg, w_act) + nt(gu, w_up)).astype(BF)
        outp[c] = nt(hidden, w_down).astype(BF)

        @pl.when(i < tp - 1)
        def _():
            send(gnp.at[c], gnr.at[i], ss.at[i], sr.at[i], {"tp": c})

        return carry

    lax.fori_loop(0, tp, chunk, 0)
    gall[0] = tn(n2[...], ggu[0]).astype(BF)
    gall[1] = tn(n2[...], ggu[1]).astype(BF)
    gall[2] = tn(cot[...], hid[...]).astype(BF)
    for o, p in enumerate(tps):
        pltpu.make_async_remote_copy(
            src_ref=gnp.at[p], dst_ref=gnr.at[o], send_sem=ss.at[o], recv_sem=sr.at[o],
            device_id={"tp": p}, device_id_type=MESH,
        ).wait()
    own = gnp[t].astype(F32)
    for o in range(tp - 1):
        own = own + gnr[o].astype(F32)
    hat, inverse = standardize(mid_rows[...])
    gain2[...] = jnp.broadcast_to(jnp.sum(own * hat, axis=0, keepdims=True), gain2.shape)
    at = pl.ds(pl.multiple_of(t * unit, unit), unit)
    gm = cot[at, :].astype(F32) + norm_back(own * gf[1:2, :], hat, inverse)
    gm_rows[...] = gm
    gml[t] = gm.astype(BF)
    copies = [
        send(gml.at[t], gml.at[t], as_.at[o], ar.at[o], {"tp": p}) for o, p in enumerate(tps)
    ]
    wo2 = nn(wo[t], spread(wo.shape[2], 384, HEAD)).astype(BF)
    for x in copies:
        x.wait()
    full = gml[...].reshape(rows, width)
    g = nn(full, wo2).astype(BF)
    for h in range(3):
        g128[h] = g[:, h * 128 : (h + 1) * 128]
    mine = mixall[t].reshape(wo.shape[2], rows)
    og = nn(mine, full).T.astype(BF)
    gall[3] = jnp.concatenate(
        [og, jnp.zeros((width, gall.shape[2] - og.shape[1]), BF)], axis=1
    )


def back_kernel(
    dp, tp, q, g, kvall, mixf, lse, outp, mid_rows, gall, tab, dq, dkv, out_rows, gfin,
    tot, dqt, buf, got, rs, orecv, dsem, drec, wsem, wrec, fsem, frec, osem, orec,
):
    rows = q.shape[1]
    d, c, t = lax.axis_index("dp"), lax.axis_index("ctx"), lax.axis_index("tp")
    sib = c + 1 - 2 * lax.rem(c, 2)
    far = lax.rem(c + 2, 4)
    diag = lax.rem(sib + 2, 4)
    others = pairs(dp, 4)
    tps = ring("tp", tp)
    ctxs = ring("ctx", 4)
    greet([{"dp": a, "ctx": b} for a, b in others] + [{"tp": p} for p in tps])
    outs = [
        send(outp.at[p], orecv.at[o], osem.at[o], orec.at[o], {"tp": p})
        for o, p in enumerate(tps)
    ]
    sums = [
        send(gall.at[b, a], rs.at[o], wsem.at[o], wrec.at[o], {"dp": a, "ctx": b})
        for o, (a, b) in enumerate(others)
    ]
    for h in range(3):
        gt = g[h].astype(F32).T[HEAD:, :]
        tot[h] = jnp.broadcast_to(jnp.sum(gt * mixf[h], axis=0, keepdims=True), (8, rows))
    dqt[...] = jnp.zeros(dqt.shape, F32)

    def block(step, b):
        def per_head(h, carry):
            def per_tile(i, inner):
                at = pl.ds(pl.multiple_of(i * 256, 256), 256)
                k = kvall[b, h, at, :]
                s = nt(k, q[h])
                p = jnp.exp(s - lse[h, 0:1, :])
                gp = nt(k, g[h])
                ds = (p * (gp - tot[h, 0:1, :])).astype(BF)
                buf[step, h, at, :] = (nn(ds, q[h]) + nn(p.astype(BF), g[h])).astype(BF)
                dqt[h] += nn(k[:, :HEAD].T, ds)
                return inner

            lax.fori_loop(0, rows // 256, per_tile, 0)
            return carry

        lax.fori_loop(0, 3, per_head, 0)

    moves = []
    for step, b in enumerate((diag, far, sib)):
        block(step, b)
        moves.append(
            send(buf.at[step], got.at[step], dsem.at[step], drec.at[step], {"ctx": b})
        )
    for x in sums:
        x.wait()
    total = gall[c, d].astype(F32)
    for o in range(len(others)):
        total = total + rs[o].astype(F32)
    gfin[c] = total.astype(BF)
    spreads = [
        send(gfin.at[c], gfin.at[c], fsem.at[o], frec.at[o], {"ctx": p})
        for o, p in enumerate(ctxs)
    ]
    block(3, c)
    r = turn(True)
    for x in outs:
        x.wait()
    own = mid_rows[...] + outp[t].astype(F32)
    for o in range(tp - 1):
        own = own + orecv[o].astype(F32)
    out_rows[...] = own.astype(BF)
    cosine, sine = tab[:, 0:128], tab[:, 128:256]
    for h in range(3):
        z = 0.125 * jnp.concatenate([dqt[h], jnp.zeros((HEAD, rows), F32)], axis=0).T
        dq[h] = (z * cosine + turned(z * sine, r)).astype(BF)
    for x in moves:
        x.wait()
    for h in range(3):
        z = buf[3, h].astype(F32)
        for o in range(3):
            z = z + got[o, h].astype(F32)
        dkv[h] = (z * cosine + turned(z * sine, r)).astype(BF)
    for x in spreads:
        x.wait()


def tail_kernel(
    dp, tp, dq, dkv, n1, tok, gm_rows, wa, gf, gain2, in_rows, gfin, gains,
    wq2, gnp, gnr, gw, rs, gb, gbt, gbc, ss, sr, wsem, wrec, fsem, frec, tsem, trec, csem, crec,
):
    rows, width = n1.shape
    unit = rows // tp
    d, c, t = lax.axis_index("dp"), lax.axis_index("ctx"), lax.axis_index("tp")
    part = width // dp
    others = pairs(dp, 4)
    tps = ring("tp", tp)
    ctxs = ring("ctx", 4)
    greet([{"dp": a, "ctx": b} for a, b in others] + [{"tp": p} for p in tps])
    wq2[...] = nn(wa[:, :256], spread(256, 384, 0)).astype(BF)

    def chunk(i, carry):
        r = lax.rem(t + 1 + i, tp)
        at = pl.ds(pl.multiple_of(r * unit, unit), unit)
        total = jnp.zeros((unit, width), F32)
        for h in range(3):
            cols = slice(h * 128, (h + 1) * 128)
            total = total + nt(dq[h, at, :], wq2[:, cols])
            total = total + nt(dkv[h, at, :], wa[:, 256 + h * 128 : 384 + h * 128])
        gnp[r] = total.astype(BF)

        @pl.when(i < tp - 1)
        def _():
            send(gnp.at[r], gnr.at[i], ss.at[i], sr.at[i], {"tp": r})

        return carry

    lax.fori_loop(0, tp, chunk, 0)
    n1t = n1[...].T
    gq = jnp.concatenate([nn(n1t, dq[h]).astype(BF) for h in range(3)], axis=1)
    gkv = jnp.concatenate([nn(n1t, dkv[h]).astype(BF) for h in range(3)], axis=1)
    low, high = gather_cols(384, 192, 0), gather_cols(384, 192, HEAD)
    gw[0] = nn(gq, low).astype(BF).reshape(dp, part, 192)
    gw[1] = nn(gkv, low).astype(BF).reshape(dp, part, 192)
    gw[2] = nn(gkv, high).astype(BF).reshape(dp, part, 192)

    def owner_copy(o, a, b):
        return pltpu.make_async_remote_copy(
            src_ref=gw.at[b, a], dst_ref=rs.at[o], send_sem=wsem.at[o], recv_sem=wrec.at[o],
            device_id={"dp": a, "ctx": b}, device_id_type=MESH,
        )

    for o, (a, b) in enumerate(others):
        @pl.when(b < 3)
        def _(o=o, a=a, b=b):
            owner_copy(o, a, b).start()

    for o, p in enumerate(tps):
        pltpu.make_async_remote_copy(
            src_ref=gnp.at[p], dst_ref=gnr.at[o], send_sem=ss.at[o], recv_sem=sr.at[o],
            device_id={"tp": p}, device_id_type=MESH,
        ).wait()
    own = gnp[t].astype(F32)
    for o in range(tp - 1):
        own = own + gnr[o].astype(F32)
    at = pl.ds(pl.multiple_of(t * unit, unit), unit)
    hat, inverse = standardize(tok[at, :].astype(F32))
    first = jnp.sum(own * hat, axis=0, keepdims=True)
    gb[...] = jnp.concatenate([first, gain2[0:1, :], jnp.zeros((6, width), F32)], axis=0)
    small = [send(gb, gbt.at[o], tsem.at[o], trec.at[o], {"tp": p}) for o, p in enumerate(tps)]
    in_rows[...] = (gm_rows[...] + norm_back(own * gf[0:1, :], hat, inverse)).astype(BF)
    for x in small:
        x.wait()
    total = gb[...]
    for o in range(tp - 1):
        total = total + gbt[o]
    gb[...] = total
    wide = [
        send(gb, gbc.at[o], csem.at[o], crec.at[o], {"dp": a, "ctx": b})
        for o, (a, b) in enumerate(others)
    ]

    @pl.when(c < 3)
    def _():
        for o, (a, b) in enumerate(others):
            owner_copy(o, a, 0).wait_recv()
        w = gw[c, d].astype(F32)
        for o in range(len(others)):
            w = w + rs[o].astype(F32)
        gfin[c] = w.astype(BF)
        for o, p in enumerate(ctxs):
            send(gfin.at[c], gfin.at[c], fsem.at[o], frec.at[o], {"ctx": p})

    for x in wide:
        x.wait()
    total = gb[...]
    for o in range(len(others)):
        total = total + gbc[o]
    gains[...] = total
    for o, (a, b) in enumerate(others):
        @pl.when(b < 3)
        def _(o=o, a=a, b=b):
            owner_copy(o, a, b).wait_send()

    def final_copy(o, p, slot):
        return pltpu.make_async_remote_copy(
            src_ref=gfin.at[slot], dst_ref=gfin.at[slot], send_sem=fsem.at[o],
            recv_sem=frec.at[o], device_id={"ctx": p}, device_id_type=MESH,
        )

    for o, p in enumerate(ctxs):
        origin = lax.rem(c + 4 - (o + 1), 4)

        @pl.when(origin < 3)
        def _(o=o, p=p, origin=origin):
            final_copy(o, p, origin).wait_recv()

    @pl.when(c < 3)
    def _():
        for o, p in enumerate(ctxs):
            final_copy(o, p, c).wait_send()


def call(kernel, number, outs, scratch, flops, *args):
    return pl.pallas_call(
        kernel,
        out_shape=[jax.ShapeDtypeStruct(s, t) for s, t in outs],
        in_specs=[VM] * len(args),
        out_specs=[VM] * len(outs),
        scratch_shapes=[
            pltpu.SemaphoreType.DMA(s) if t is None else pltpu.VMEM(s, t) for s, t in scratch
        ],
        compiler_params=pltpu.CompilerParams(
            collective_id=number, has_side_effects=True, vmem_limit_bytes=56 * 2**20
        ),
        cost_estimate=pl.CostEstimate(flops=flops, bytes_accessed=10**7, transcendentals=0),
    )(*args)


def local(
    dp, ctx, tp, tokens, w_query, w_key, w_value, w_out, w_act, w_up, w_down, gain_one, gain_two,
    cotangent,
):
    T, D = tokens.shape
    part = w_query.shape[0]
    feat = w_query.shape[1]
    hidden = w_act.shape[1]
    unit = T // tp
    pad = jnp.zeros((part, HEAD), BF)
    mixed = [w_query, pad]
    for h in range(3):
        at = slice(h * HEAD, (h + 1) * HEAD)
        mixed += [w_key[:, at], w_value[:, at]]
    pa = jnp.concatenate(mixed, axis=1)
    gn = jnp.concatenate([gain_one[None], gain_two[None], jnp.zeros((14, part), BF)], axis=0)
    pb = jnp.stack([w_act, w_up, w_down.T])
    pc = w_out.T
    position = np.arange(ctx * T, dtype=np.float32)
    frequency = (ROPE_BASE ** (-np.arange(0, HEAD, 2) / HEAD)).astype(np.float32)
    angle = (position[:, None] * frequency[None, :]).astype(np.float64)
    cosine, sine = np.cos(angle), np.sin(angle)
    table = np.concatenate(
        [cosine, cosine, np.ones((ctx * T, HEAD)), sine, sine, np.zeros((ctx * T, HEAD))], axis=1
    ).astype(np.float32)
    tab = lax.dynamic_slice_in_dim(jnp.asarray(table), lax.axis_index("ctx") * T, T, 0)
    n_d, n_t, n_dt, n_dc = dp - 1, tp - 1, dp * tp - 1, dp * ctx - 1
    q, kv, wa, gf, n1 = call(
        functools.partial(project_kernel, dp), 1,
        [((3, T, 128), BF), ((3, T, 128), BF), ((dp, part, 640), BF), ((16, D), F32), ((T, D), BF)],
        [((dp, 16, part), BF), ((D, 384), BF)] + [((n_d,), None)] * 4, 10**9,
        tokens, pa, gn, tab,
    )
    kvall, mixall, mixf, lse, wb, wo = call(
        functools.partial(attend_kernel, dp, tp), 2,
        [
            ((ctx, 3, T, 128), BF), ((tp, 3, HEAD, T), BF), ((3, HEAD, T), F32), ((3, 8, T), F32),
            ((dp, 3, part, hidden), BF), ((tp, dp, part, feat), BF),
        ],
        [((3, 8, T), F32), ((3, 8, T), F32), ((3, HEAD, T), F32), ((HEAD, T), BF)]
        + [((3,), None)] * 2 + [((n_d,), None)] * 2 + [((n_dt,), None)] * 2
        + [((n_t, 3), None)] * 2, 10**10,
        q, kv, pb, pc,
    )
    wb = jnp.transpose(wb, (1, 0, 2, 3)).reshape(3, D, hidden)
    wo = wo.reshape(tp, D, feat)
    outp, mid_rows, gm_rows, g128, gall, gain2 = call(
        functools.partial(feed_kernel, tp), 3,
        [
            ((tp, unit, D), BF), ((unit, D), F32), ((unit, D), F32), ((3, T, 128), BF),
            ((4, D, hidden), BF), ((8, D), F32),
        ],
        [
            ((T, D), BF), ((2, T, hidden), BF), ((T, hidden), BF), ((tp, unit, D), BF),
            ((n_t, unit, D), BF), ((tp, unit, D), BF),
        ] + [((n_t,), None)] * 4, 10**10,
        tokens, mixall, wo, wb, gf, cotangent,
    )
    dq, dkv, out_rows, gfin = call(
        functools.partial(back_kernel, dp, tp), 4,
        [((3, T, 128), BF), ((3, T, 128), BF), ((unit, D), BF), ((4, part, hidden), BF)],
        [
            ((3, 8, T), F32), ((3, HEAD, T), F32), ((4, 3, T, 128), BF), ((3, 3, T, 128), BF),
            ((n_dc, part, hidden), BF), ((n_t, unit, D), BF),
        ] + [((3,), None)] * 2 + [((n_dc,), None)] * 2 + [((3,), None)] * 2 + [((n_t,), None)] * 2,
        10**10,
        q, g128, kvall, mixf, lse, outp, mid_rows, gall.reshape(4, dp, part, hidden), tab,
    )
    in_rows, gqkv, gains = call(
        functools.partial(tail_kernel, dp, tp), 5,
        [((unit, D), BF), ((3, part, feat), BF), ((8, D), F32)],
        [
            ((D, 384), BF), ((tp, unit, D), BF), ((n_t, unit, D), BF), ((3, dp, part, feat), BF),
            ((n_dc, part, feat), BF), ((8, D), F32), ((n_t, 8, D), F32), ((n_dc, 8, D), F32),
        ] + [((n_t,), None)] * 2 + [((n_dc,), None)] * 2 + [((3,), None)] * 2
        + [((n_t,), None)] * 2 + [((n_dc,), None)] * 2, 10**10,
        dq, dkv, n1, tokens, gm_rows, wa.reshape(D, 640), gf, gain2,
    )
    own = lax.dynamic_slice_in_dim(gains[:2], lax.axis_index("dp") * part, part, 1)
    return (
        out_rows,
        in_rows,
        gqkv[0].astype(F32),
        gqkv[1].astype(F32),
        gqkv[2].astype(F32),
        gfin[3][:, :feat].T.astype(F32),
        gfin[0].astype(F32),
        gfin[1].astype(F32),
        gfin[2].T.astype(F32),
        own[0],
        own[1],
    )


def solution(mesh):
    in_specs = (
        P(("dp", "ctx"), None),
        P("dp", "tp"),
        P("dp", "tp"),
        P("dp", "tp"),
        P("tp", "dp"),
        P("dp", "tp"),
        P("dp", "tp"),
        P("tp", "dp"),
        P("dp"),
        P("dp"),
        P(("dp", "ctx"), None),
    )
    out_specs = (
        P(("dp", "ctx", "tp"), None),
        P(("dp", "ctx", "tp"), None),
        P("dp", "tp"),
        P("dp", "tp"),
        P("dp", "tp"),
        P("tp", "dp"),
        P("dp", "tp"),
        P("dp", "tp"),
        P("tp", "dp"),
        P("dp"),
        P("dp"),
    )
    body = functools.partial(local, mesh.shape["dp"], mesh.shape["ctx"], mesh.shape["tp"])
    return jax.shard_map(body, mesh=mesh, in_specs=in_specs, out_specs=out_specs, check_vma=False)
```

```python
import functools
import math

import jax
import jax.numpy as jnp
import numpy as np
from jax import lax
from jax.experimental import pallas as pl
from jax.experimental.pallas import tpu as pltpu
from jax.sharding import PartitionSpec as P

HEAD = 64
EPSILON = 1e-05
ROPE_BASE = 160000.0
MESH = pl.DeviceIdType.MESH
BF = jnp.bfloat16
F32 = jnp.float32
VM = pl.BlockSpec(memory_space=pltpu.VMEM)


def nn(a, b):
    return lax.dot_general(a, b, (((1,), (0,)), ((), ())), preferred_element_type=F32)


def nt(a, b):
    return lax.dot_general(a, b, (((1,), (1,)), ((), ())), preferred_element_type=F32)


def tn(a, b):
    return lax.dot_general(a, b, (((0,), (0,)), ((), ())), preferred_element_type=F32)


def iotas(rows, cols):
    return (
        lax.broadcasted_iota(jnp.int32, (rows, cols), 0),
        lax.broadcasted_iota(jnp.int32, (rows, cols), 1),
    )


def spread(rows, cols, shift):
    i, j = iotas(rows, cols)
    return (j == (i // HEAD) * 128 + i % HEAD + shift).astype(BF)


def gather_cols(rows, cols, shift):
    i, j = iotas(rows, cols)
    return (i == (j // HEAD) * 128 + j % HEAD + shift).astype(BF)


def turn(back):
    i, j = iotas(128, 128)
    if back:
        i, j = j, i
    half = HEAD // 2
    plus = (i == j - half) & (j < HEAD)
    minus = (i == j + half) & (i < HEAD)
    return jnp.where(plus, 1.0, jnp.where(minus, -1.0, 0.0)).astype(BF)


def turned(z, r):
    high = z.astype(BF)
    rest = (z - high.astype(F32)).astype(BF)
    return nn(high, r) + nn(rest, r)


def standardize(x):
    mean_value = jnp.mean(x, axis=-1, keepdims=True)
    centred = x - mean_value
    inverse = lax.rsqrt(jnp.mean(centred * centred, axis=-1, keepdims=True) + EPSILON)
    return centred * inverse, inverse


def norm_back(grad_hat, hat, inverse):
    mean_grad = jnp.mean(grad_hat, axis=-1, keepdims=True)
    mean_cross = jnp.mean(grad_hat * hat, axis=-1, keepdims=True)
    return inverse * (grad_hat - mean_grad - hat * mean_cross)


def greet(peers):
    barrier = pltpu.get_barrier_semaphore()
    for peer in peers:
        pl.semaphore_signal(barrier, inc=1, device_id=peer, device_id_type=MESH)
    pl.semaphore_wait(barrier, len(peers))


def send(src, dst, s_sem, r_sem, peer):
    copy = pltpu.make_async_remote_copy(
        src_ref=src, dst_ref=dst, send_sem=s_sem, recv_sem=r_sem, device_id=peer, device_id_type=MESH
    )
    copy.start()
    return copy


def ring(axis, count):
    me = lax.axis_index(axis)
    return [lax.rem(me + o, count) for o in range(1, count)]


def pairs(dp, ctx):
    d, c = lax.axis_index("dp"), lax.axis_index("ctx")
    return [
        (lax.rem(d + od, dp), lax.rem(c + oc, ctx))
        for od in range(dp)
        for oc in range(ctx)
        if od or oc
    ]


def project_kernel(
    dp, tok, pa, gn, tab, q_out, kv_out, wa, gf, n1, gslot, wq2, gs, gr, ws, wr
):
    rows = tok.shape[0]
    width = tok.shape[1]
    part = pa.shape[0]
    me = lax.axis_index("dp")
    peers = ring("dp", dp)
    greet([{"dp": p} for p in peers])
    copies = []
    for o, p in enumerate(peers):
        copies.append(send(gn, gslot.at[me], gs.at[o], gr.at[o], {"dp": p}))
    weights = []
    for o, p in enumerate(peers):
        weights.append(send(pa, wa.at[me], ws.at[o], wr.at[o], {"dp": p}))
    wa[me] = pa[...]
    gslot[me] = gn[...]
    for c in copies:
        c.wait()
    gains = jnp.zeros((16, width), F32)
    for d in range(dp):
        i, j = iotas(part, width)
        gains = gains + nn(gslot[d], (j == i + d * part).astype(BF))
    gf[...] = gains

    def norm_rows(i, carry):
        at = pl.ds(pl.multiple_of(i * 128, 128), 128)
        hat, _ = standardize(tok[at, :].astype(F32))
        n1[at, :] = (hat * gf[0:1, :]).astype(BF)
        return carry

    lax.fori_loop(0, rows // 128, norm_rows, 0)
    for c in weights:
        c.wait()
    whole = wa[...].reshape(width, wa.shape[2])
    wq2[...] = nn(whole[:, :256], spread(256, 384, 0)).astype(BF)
    r = turn(False)

    def chunk(i, carry):
        at = pl.ds(pl.multiple_of(i * 256, 256), 256)
        x = n1[at, :]
        zq = nn(x, wq2[...])
        zk = nn(x, wa[...].reshape(width, wa.shape[2])[:, 256:])
        cosine, sine = tab[at, 0:128], tab[at, 128:256]
        for h in range(3):
            a = zq[:, h * 128 : (h + 1) * 128]
            q_out[h, at, :] = (0.125 * (a * cosine + turned(a, r) * sine)).astype(BF)
            b = zk[:, h * 128 : (h + 1) * 128]
            kv_out[h, at, :] = (b * cosine + turned(b, r) * sine).astype(BF)
        return carry

    lax.fori_loop(0, rows // 256, chunk, 0)


def attend_kernel(
    dp, tp, q, kv, pb, pc, kvall, mixall, mixf, lse, wb, wo,
    m_s, l_s, acc, vt, ks, kr, bs, br, cs, cr, ts, tr,
):
    rows = q.shape[1]
    d, c, t = lax.axis_index("dp"), lax.axis_index("ctx"), lax.axis_index("tp")
    sib = c + 1 - 2 * lax.rem(c, 2)
    far = lax.rem(c + 2, 4)
    diag = lax.rem(sib + 2, 4)
    dps = ring("dp", dp)
    both = [
        (lax.rem(d + od, dp), lax.rem(t + ot, tp))
        for od in range(dp)
        for ot in range(tp)
        if od or ot
    ]
    greet(
        [{"ctx": sib}, {"ctx": far}] + [{"dp": a, "tp": b} for a, b in both]
    )
    to_far = send(kv, kvall.at[c], ks.at[1], kr.at[1], {"ctx": far})
    to_sib = send(kv, kvall.at[c], ks.at[0], kr.at[0], {"ctx": sib})
    copies = []
    for o, (a, b) in enumerate(both):
        copies.append(send(pc, wo.at[t, d], cs.at[o], cr.at[o], {"dp": a, "tp": b}))
    for o, a in enumerate(dps):
        copies.append(send(pb, wb.at[:, d], bs.at[o], br.at[o], {"dp": a}))
    wo[t, d] = pc[...]
    for m in range(3):
        wb[m, d] = pb[m]
    kvall[c] = kv[...]
    m_s[...] = jnp.full(m_s.shape, -1e30, F32)
    l_s[...] = jnp.zeros(l_s.shape, F32)
    acc[...] = jnp.zeros(acc.shape, F32)
    tps = ring("tp", tp)

    def block(*steps):
        def per_head(h, carry):
            for step, b in steps:
                one(step, b, h)
            if steps[-1][0] == 3:
                for o, p in enumerate(tps):
                    send(
                        mixall.at[t, h], mixall.at[t, h], ts.at[o, h], tr.at[o, h], {"tp": p}
                    )
            return carry

        def one(step, b, h):
            vt[...] = kvall[b, h][:, HEAD:].T

            def per_tile(i, inner):
                at = pl.ds(pl.multiple_of(i * 256, 256), 256)
                s = nt(kvall[b, h], q[h, at, :])
                old = m_s[h, 0:1, at]
                new = jnp.maximum(old, jnp.max(s, axis=0, keepdims=True))
                p = jnp.exp(s - new)
                shrink = jnp.exp(old - new)
                m_s[h, 0:1, at] = new
                total = l_s[h, 0:1, at] * shrink + jnp.sum(p, axis=0, keepdims=True)
                l_s[h, 0:1, at] = total
                fresh = acc[h, :, at] * shrink + nn(vt[...], p.astype(BF))
                if step < 3:
                    acc[h, :, at] = fresh
                else:
                    mix = fresh / total
                    mixf[h, :, at] = mix
                    mixall[t, h, :, at] = mix.astype(BF)
                    lse[h, :, at] = jnp.broadcast_to(new + jnp.log(total), (8, 256))
                return inner

            lax.fori_loop(0, rows // 256, per_tile, 0)

        lax.fori_loop(0, 3, per_head, 0)

    block((0, c))
    to_sib.wait_recv()
    to_far.wait_recv()
    onward = send(kvall.at[far], kvall.at[far], ks.at[2], kr.at[2], {"ctx": sib})
    block((1, sib))
    onward.wait_recv()
    block((2, far), (3, diag))
    to_far.wait_send()
    to_sib.wait_send()
    onward.wait_send()
    for x in copies:
        x.wait()
    for h in range(3):
        for o, p in enumerate(tps):
            pltpu.make_async_remote_copy(
                src_ref=mixall.at[t, h], dst_ref=mixall.at[t, h], send_sem=ts.at[o, h],
                recv_sem=tr.at[o, h], device_id={"tp": p}, device_id_type=MESH,
            ).wait()


def feed_kernel(
    tp, tok, mixall, wo, wb, gf, cot, outp, mid_rows, gm_rows, g128, gall, gain2, gml,
    n2, ggu, hid, gnp, gnr, gsend, wo2, ss, sr, as_, ar,
):
    rows, width = tok.shape
    unit = rows // tp
    t = lax.axis_index("tp")
    tps = ring("tp", tp)
    greet([{"tp": p} for p in tps])

    def chunk(i, carry):
        c = lax.rem(t + 1 + i, tp)
        at = pl.ds(pl.multiple_of(c * unit, unit), unit)
        middle = tok[at, :].astype(F32)
        for k in range(tp):
            m = mixall[k, :, :, at].reshape(wo.shape[2], unit).T
            middle = middle + nt(m, wo[k])
        mid_rows[...] = middle
        hat, _ = standardize(middle)
        x = (hat * gf[1:2, :]).astype(BF)
        n2[at, :] = x
        w_act, w_up, w_down = wb[0], wb[1], wb[2]
        gate = nn(x, w_act)
        up = nn(x, w_up)
        gh = nn(cot[at, :], w_down)
        cdf = 0.5 * (1.0 + lax.erf(gate * (1.0 / math.sqrt(2.0))))
        density = jnp.exp(-0.5 * gate * gate) * (1.0 / math.sqrt(2.0 * math.pi))
        active = gate * cdf
        hidden = (active * up).astype(BF)
        hid[at, :] = hidden
        gg = (gh * up * (cdf + gate * density)).astype(BF)
        gu = (gh * active).astype(BF)
        ggu[0, at, :] = gg
        ggu[1, at, :] = gu
        gnp[c] = (nt(gg, w_act) + nt(gu, w_up)).astype(BF)
        outp[c] = nt(hidden, w_down).astype(BF)

        @pl.when(i < tp - 1)
        def _():
            send(gnp.at[c], gnr.at[i], ss.at[i], sr.at[i], {"tp": c})

        return carry

    lax.fori_loop(0, tp, chunk, 0)
    gall[0] = tn(n2[...], ggu[0]).astype(BF)
    gall[1] = tn(n2[...], ggu[1]).astype(BF)
    gall[2] = tn(cot[...], hid[...]).astype(BF)
    for o, p in enumerate(tps):
        pltpu.make_async_remote_copy(
            src_ref=gnp.at[p], dst_ref=gnr.at[o], send_sem=ss.at[o], recv_sem=sr.at[o],
            device_id={"tp": p}, device_id_type=MESH,
        ).wait()
    own = gnp[t].astype(F32)
    for o in range(tp - 1):
        own = own + gnr[o].astype(F32)
    hat, inverse = standardize(mid_rows[...])
    gain2[...] = jnp.broadcast_to(jnp.sum(own * hat, axis=0, keepdims=True), gain2.shape)
    at = pl.ds(pl.multiple_of(t * unit, unit), unit)
    gm = cot[at, :].astype(F32) + norm_back(own * gf[1:2, :], hat, inverse)
    gm_rows[...] = gm
    gml[...] = gm.astype(BF)
    copies = []
    for o in list(range(1, tp)) + [0]:
        p = lax.rem(t + o, tp)
        gsend[p] = nn(gml[...], wo[p]).astype(BF)
        if o:
            copies.append(
                send(gsend.at[p], wo2.at[t], as_.at[o - 1], ar.at[o - 1], {"tp": p})
            )
    wo2[t] = gsend[t]
    spacing = spread(wo.shape[2], 384, HEAD)
    for x in copies:
        x.wait()
    g = nn(wo2[...].reshape(rows, wo.shape[2]), spacing).astype(BF)
    for h in range(3):
        g128[h] = g[:, h * 128 : (h + 1) * 128]


def back_kernel(
    dp, tp, q, g, kvall, mixf, lse, outp, mid_rows, gall, tab, gml, dq, dkv, out_rows, gfin, gmlall,
    tot, dqt, buf, got, rs, orecv, dsem, drec, wsem, wrec, fsem, frec, osem, orec, asem, arec,
):
    rows = q.shape[1]
    d, c, t = lax.axis_index("dp"), lax.axis_index("ctx"), lax.axis_index("tp")
    sib = c + 1 - 2 * lax.rem(c, 2)
    far = lax.rem(c + 2, 4)
    diag = lax.rem(sib + 2, 4)
    others = pairs(dp, 4)
    tps = ring("tp", tp)
    ctxs = ring("ctx", 4)
    greet([{"dp": a, "ctx": b} for a, b in others] + [{"tp": p} for p in tps])
    outs = [
        send(outp.at[p], orecv.at[o], osem.at[o], orec.at[o], {"tp": p})
        for o, p in enumerate(tps)
    ]
    outs += [
        send(gml, gmlall.at[t], asem.at[o], arec.at[o], {"tp": p}) for o, p in enumerate(tps)
    ]
    gmlall[t] = gml[...]

    def owner_copy(o, a, b):
        return pltpu.make_async_remote_copy(
            src_ref=gall.at[b, a], dst_ref=rs.at[o], send_sem=wsem.at[o], recv_sem=wrec.at[o],
            device_id={"dp": a, "ctx": b}, device_id_type=MESH,
        )

    for o, (a, b) in enumerate(others):
        @pl.when(b < 3)
        def _(o=o, a=a, b=b):
            owner_copy(o, a, b).start()

    for h in range(3):
        gt = g[h].astype(F32).T[HEAD:, :]
        tot[h] = jnp.broadcast_to(jnp.sum(gt * mixf[h], axis=0, keepdims=True), (8, rows))
    dqt[...] = jnp.zeros(dqt.shape, F32)

    def block(step, b):
        def per_head(h, carry):
            def per_tile(i, inner):
                at = pl.ds(pl.multiple_of(i * 256, 256), 256)
                k = kvall[b, h, at, :]
                s = nt(k, q[h])
                p = jnp.exp(s - lse[h, 0:1, :])
                gp = nt(k, g[h])
                ds = (p * (gp - tot[h, 0:1, :])).astype(BF)
                buf[step, h, at, :] = (nn(ds, q[h]) + nn(p.astype(BF), g[h])).astype(BF)
                dqt[h] += nn(k[:, :HEAD].T, ds)
                return inner

            lax.fori_loop(0, rows // 256, per_tile, 0)
            return carry

        lax.fori_loop(0, 3, per_head, 0)

    moves = []
    for step, b in enumerate((diag, far, sib)):
        block(step, b)
        moves.append(
            send(buf.at[step], got.at[step], dsem.at[step], drec.at[step], {"ctx": b})
        )
    @pl.when(c < 3)
    def _():
        for o, (a, b) in enumerate(others):
            owner_copy(o, a, 0).wait_recv()
        total = gall[c, d].astype(F32)
        for o in range(len(others)):
            total = total + rs[o].astype(F32)
        gfin[c] = total.astype(BF)
        for o, p in enumerate(ctxs):
            send(gfin.at[c], gfin.at[c], fsem.at[o], frec.at[o], {"ctx": p})

    block(3, c)
    r = turn(True)
    for x in outs:
        x.wait()
    own = mid_rows[...] + outp[t].astype(F32)
    for o in range(tp - 1):
        own = own + orecv[o].astype(F32)
    out_rows[...] = own.astype(BF)
    cosine, sine = tab[:, 0:128], tab[:, 128:256]
    for h in range(3):
        z = 0.125 * jnp.concatenate([dqt[h], jnp.zeros((HEAD, rows), F32)], axis=0).T
        dq[h] = (z * cosine + turned(z * sine, r)).astype(BF)
    for x in moves:
        x.wait()
    for h in range(3):
        z = buf[3, h].astype(F32)
        for o in range(3):
            z = z + got[o, h].astype(F32)
        dkv[h] = (z * cosine + turned(z * sine, r)).astype(BF)
    for o, (a, b) in enumerate(others):
        @pl.when(b < 3)
        def _(o=o, a=a, b=b):
            owner_copy(o, a, b).wait_send()

    def final_copy(o, p, slot):
        return pltpu.make_async_remote_copy(
            src_ref=gfin.at[slot], dst_ref=gfin.at[slot], send_sem=fsem.at[o],
            recv_sem=frec.at[o], device_id={"ctx": p}, device_id_type=MESH,
        )

    for o, p in enumerate(ctxs):
        origin = lax.rem(c + 4 - (o + 1), 4)

        @pl.when(origin < 3)
        def _(o=o, p=p, origin=origin):
            final_copy(o, p, origin).wait_recv()

    @pl.when(c < 3)
    def _():
        for o, p in enumerate(ctxs):
            final_copy(o, p, c).wait_send()


def tail_kernel(
    dp, tp, dq, dkv, n1, tok, gm_rows, wa, gf, gain2, mixall, gml, in_rows, gfin, gains,
    wq2, gnp, gnr, gw, rs, gb, gbt, gbc, ss, sr, wsem, wrec, fsem, frec, tsem, trec, csem, crec,
):
    rows, width = n1.shape
    unit = rows // tp
    d, c, t = lax.axis_index("dp"), lax.axis_index("ctx"), lax.axis_index("tp")
    part = width // dp
    others = pairs(dp, 4)
    tps = ring("tp", tp)
    ctxs = ring("ctx", 4)
    greet([{"dp": a, "ctx": b} for a, b in others] + [{"tp": p} for p in tps])
    wq2[...] = nn(wa[:, :256], spread(256, 384, 0)).astype(BF)

    def chunk(i, carry):
        r = lax.rem(t + 1 + i, tp)
        at = pl.ds(pl.multiple_of(r * unit, unit), unit)
        total = jnp.zeros((unit, width), F32)
        for h in range(3):
            cols = slice(h * 128, (h + 1) * 128)
            total = total + nt(dq[h, at, :], wq2[:, cols])
            total = total + nt(dkv[h, at, :], wa[:, 256 + h * 128 : 384 + h * 128])
        gnp[r] = total.astype(BF)

        @pl.when(i < tp - 1)
        def _():
            send(gnp.at[r], gnr.at[i], ss.at[i], sr.at[i], {"tp": r})

        return carry

    lax.fori_loop(0, tp, chunk, 0)
    n1t = n1[...].T
    gq = jnp.concatenate([nn(n1t, dq[h]).astype(BF) for h in range(3)], axis=1)
    gkv = jnp.concatenate([nn(n1t, dkv[h]).astype(BF) for h in range(3)], axis=1)
    low, high = gather_cols(384, 192, 0), gather_cols(384, 192, HEAD)
    gw[0] = nn(gq, low).astype(BF).reshape(dp, part, 192)
    gw[1] = nn(gkv, low).astype(BF).reshape(dp, part, 192)
    gw[2] = nn(gkv, high).astype(BF).reshape(dp, part, 192)
    mine = mixall[t].reshape(192, rows)
    gw[3] = nn(mine, gml[...].reshape(rows, width)).T.astype(BF).reshape(dp, part, 192)

    sums = [
        send(gw.at[b, a], rs.at[o], wsem.at[o], wrec.at[o], {"dp": a, "ctx": b})
        for o, (a, b) in enumerate(others)
    ]
    for x in sums:
        x.wait()
    w = gw[c, d].astype(F32)
    for o in range(len(others)):
        w = w + rs[o].astype(F32)
    gfin[c] = w.astype(BF)
    spreads = [
        send(gfin.at[c], gfin.at[c], fsem.at[o], frec.at[o], {"ctx": p})
        for o, p in enumerate(ctxs)
    ]
    for o, p in enumerate(tps):
        pltpu.make_async_remote_copy(
            src_ref=gnp.at[p], dst_ref=gnr.at[o], send_sem=ss.at[o], recv_sem=sr.at[o],
            device_id={"tp": p}, device_id_type=MESH,
        ).wait()
    own = gnp[t].astype(F32)
    for o in range(tp - 1):
        own = own + gnr[o].astype(F32)
    at = pl.ds(pl.multiple_of(t * unit, unit), unit)
    hat, inverse = standardize(tok[at, :].astype(F32))
    first = jnp.sum(own * hat, axis=0, keepdims=True)
    gb[...] = jnp.concatenate([first, gain2[0:1, :], jnp.zeros((6, width), F32)], axis=0)
    small = [send(gb, gbt.at[o], tsem.at[o], trec.at[o], {"tp": p}) for o, p in enumerate(tps)]
    in_rows[...] = (gm_rows[...] + norm_back(own * gf[0:1, :], hat, inverse)).astype(BF)
    for x in small:
        x.wait()
    total = gb[...]
    for o in range(tp - 1):
        total = total + gbt[o]
    gb[...] = total
    wide = [
        send(gb, gbc.at[o], csem.at[o], crec.at[o], {"dp": a, "ctx": b})
        for o, (a, b) in enumerate(others)
    ]
    for x in wide:
        x.wait()
    total = gb[...]
    for o in range(len(others)):
        total = total + gbc[o]
    gains[...] = total
    for x in spreads:
        x.wait()


def call(kernel, number, outs, scratch, flops, *args):
    return pl.pallas_call(
        kernel,
        out_shape=[jax.ShapeDtypeStruct(s, t) for s, t in outs],
        in_specs=[VM] * len(args),
        out_specs=[VM] * len(outs),
        scratch_shapes=[
            pltpu.SemaphoreType.DMA(s) if t is None else pltpu.VMEM(s, t) for s, t in scratch
        ],
        compiler_params=pltpu.CompilerParams(
            collective_id=number, has_side_effects=True, vmem_limit_bytes=56 * 2**20
        ),
        cost_estimate=pl.CostEstimate(flops=flops, bytes_accessed=10**7, transcendentals=0),
    )(*args)


def local(
    dp, ctx, tp, tokens, w_query, w_key, w_value, w_out, w_act, w_up, w_down, gain_one, gain_two,
    cotangent,
):
    T, D = tokens.shape
    part = w_query.shape[0]
    feat = w_query.shape[1]
    hidden = w_act.shape[1]
    unit = T // tp
    pad = jnp.zeros((part, HEAD), BF)
    mixed = [w_query, pad]
    for h in range(3):
        at = slice(h * HEAD, (h + 1) * HEAD)
        mixed += [w_key[:, at], w_value[:, at]]
    pa = jnp.concatenate(mixed, axis=1)
    gn = jnp.concatenate([gain_one[None], gain_two[None], jnp.zeros((14, part), BF)], axis=0)
    pb = jnp.stack([w_act, w_up, w_down.T])
    pc = w_out.T
    position = np.arange(ctx * T, dtype=np.float32)
    frequency = (ROPE_BASE ** (-np.arange(0, HEAD, 2) / HEAD)).astype(np.float32)
    angle = (position[:, None] * frequency[None, :]).astype(np.float64)
    cosine, sine = np.cos(angle), np.sin(angle)
    table = np.concatenate(
        [cosine, cosine, np.ones((ctx * T, HEAD)), sine, sine, np.zeros((ctx * T, HEAD))], axis=1
    ).astype(np.float32)
    tab = lax.dynamic_slice_in_dim(jnp.asarray(table), lax.axis_index("ctx") * T, T, 0)
    n_d, n_t, n_dt, n_dc = dp - 1, tp - 1, dp * tp - 1, dp * ctx - 1
    q, kv, wa, gf, n1 = call(
        functools.partial(project_kernel, dp), 1,
        [((3, T, 128), BF), ((3, T, 128), BF), ((dp, part, 640), BF), ((16, D), F32), ((T, D), BF)],
        [((dp, 16, part), BF), ((D, 384), BF)] + [((n_d,), None)] * 4, 10**9,
        tokens, pa, gn, tab,
    )
    kvall, mixall, mixf, lse, wb, wo = call(
        functools.partial(attend_kernel, dp, tp), 2,
        [
            ((ctx, 3, T, 128), BF), ((tp, 3, HEAD, T), BF), ((3, HEAD, T), F32), ((3, 8, T), F32),
            ((3, dp, part, hidden), BF), ((tp, dp, part, feat), BF),
        ],
        [((3, 8, T), F32), ((3, 8, T), F32), ((3, HEAD, T), F32), ((HEAD, T), BF)]
        + [((3,), None)] * 2 + [((n_d,), None)] * 2 + [((n_dt,), None)] * 2
        + [((n_t, 3), None)] * 2, 10**10,
        q, kv, pb, pc,
    )
    wb = wb.reshape(3, D, hidden)
    wo = wo.reshape(tp, D, feat)
    outp, mid_rows, gm_rows, g128, gall, gain2, gml = call(
        functools.partial(feed_kernel, tp), 3,
        [
            ((tp, unit, D), BF), ((unit, D), F32), ((unit, D), F32), ((3, T, 128), BF),
            ((3, D, hidden), BF), ((8, D), F32), ((unit, D), BF),
        ],
        [
            ((T, D), BF), ((2, T, hidden), BF), ((T, hidden), BF), ((tp, unit, D), BF),
            ((n_t, unit, D), BF), ((tp, unit, feat), BF), ((tp, unit, feat), BF),
        ] + [((n_t,), None)] * 4, 10**10,
        tokens, mixall, wo, wb, gf, cotangent,
    )
    dq, dkv, out_rows, gfin, gmlall = call(
        functools.partial(back_kernel, dp, tp), 4,
        [((3, T, 128), BF), ((3, T, 128), BF), ((unit, D), BF), ((3, part, hidden), BF), ((tp, unit, D), BF)],
        [
            ((3, 8, T), F32), ((3, HEAD, T), F32), ((4, 3, T, 128), BF), ((3, 3, T, 128), BF),
            ((n_dc, part, hidden), BF), ((n_t, unit, D), BF),
        ] + [((3,), None)] * 2 + [((n_dc,), None)] * 2 + [((3,), None)] * 2 + [((n_t,), None)] * 4,
        10**10,
        q, g128, kvall, mixf, lse, outp, mid_rows, gall.reshape(3, dp, part, hidden), tab, gml,
    )
    in_rows, gqkv, gains = call(
        functools.partial(tail_kernel, dp, tp), 5,
        [((unit, D), BF), ((4, part, feat), BF), ((8, D), F32)],
        [
            ((D, 384), BF), ((tp, unit, D), BF), ((n_t, unit, D), BF), ((4, dp, part, feat), BF),
            ((n_dc, part, feat), BF), ((8, D), F32), ((n_t, 8, D), F32), ((n_dc, 8, D), F32),
        ] + [((n_t,), None)] * 2 + [((n_dc,), None)] * 2 + [((3,), None)] * 2
        + [((n_t,), None)] * 2 + [((n_dc,), None)] * 2, 10**10,
        dq, dkv, n1, tokens, gm_rows, wa.reshape(D, 640), gf, gain2, mixall, gmlall,
    )
    own = lax.dynamic_slice_in_dim(gains[:2], lax.axis_index("dp") * part, part, 1)
    return (
        out_rows,
        in_rows,
        gqkv[0].astype(F32),
        gqkv[1].astype(F32),
        gqkv[2].astype(F32),
        gqkv[3].T.astype(F32),
        gfin[0].astype(F32),
        gfin[1].astype(F32),
        gfin[2].T.astype(F32),
        own[0],
        own[1],
    )


def solution(mesh):
    in_specs = (
        P(("dp", "ctx"), None),
        P("dp", "tp"),
        P("dp", "tp"),
        P("dp", "tp"),
        P("tp", "dp"),
        P("dp", "tp"),
        P("dp", "tp"),
        P("tp", "dp"),
        P("dp"),
        P("dp"),
        P(("dp", "ctx"), None),
    )
    out_specs = (
        P(("dp", "ctx", "tp"), None),
        P(("dp", "ctx", "tp"), None),
        P("dp", "tp"),
        P("dp", "tp"),
        P("dp", "tp"),
        P("tp", "dp"),
        P("dp", "tp"),
        P("dp", "tp"),
        P("tp", "dp"),
        P("dp"),
        P("dp"),
    )
    body = functools.partial(local, mesh.shape["dp"], mesh.shape["ctx"], mesh.shape["tp"])
    return jax.shard_map(body, mesh=mesh, in_specs=in_specs, out_specs=out_specs, check_vma=False)
```
